128 devices in a mesh: rep: 16 (over y_hi, z, core), fsdp: 8 (over y_lo, x).
Axes of the slice: x: 4, y: 4 (y_hi: 2, y_lo: 2; y = y_hi * 2 + y_lo), z: 4, core: 2. Of those that a mesh axis runs over, the one named last changes fastest.
Arguments:
- hidden_in: float32 [16, 1024, 1024], P('rep', 'fsdp'), may hold values from -6 to 6
- cotangent: float32 [16, 1024, 1024], P('rep', 'fsdp'), may hold values from -6 to 6
- units: bfloat16 [96, 1024, 128], P('fsdp'), may hold values from -0.70710678 to 0.70710678
- unit_momentum: float32 [96, 1024, 128], P('fsdp'), may hold values from -230.4 to 230.4
- small: float32 [37192], replicated, may hold values from -6.5 to 2
- small_momentum: float32 [37192], replicated, may hold values from -230.4 to 230.4
Outputs:
- output: float32 [16, 1024, 1024], P('rep', 'fsdp')
- grad_input: float32 [16, 1024, 1024], P('rep', 'fsdp')
- units_new: float32 [96, 1024, 128], P('fsdp')
- momentum_new: float32 [96, 1024, 128], P('fsdp')
- small_new: float32 [37192], replicated
- small_momentum_new: float32 [37192], replicated
The draws below stay inside these ranges and needn't reach their ends.
All inputs are finite; a program needn't handle non-finite values.
Results may differ from the reference program's by a relative error of at most 0.023.
Values may be sent and summed in bfloat16 or wider, within the bound.
A program may use at most 192 MiB of HBM per device.

```python
import math
import jax
import jax.numpy as jnp
import numpy as np
from jax import lax

D = 1024
INNER_WIDTH = 1536
HM = 24
HP = 64
DS = 128
KW = 4
QUERY_HEADS = 8
KEY_VALUE_HEADS = 2
HEAD_SIZE = 64
FF = 2048
UCOL = 128
LEN = 1024
MIX_IN = 4096
CONV_CHANNELS = 1792
UNITS = 96
SMALL = 37192
SPAN = 128
NSEQ = 16
TOKENS = 16384


def draw_units(key, part):
    key = jax.random.fold_in(key, 11)
    counts = [(MIX_IN + 2 * FF) // UCOL, INNER_WIDTH // UCOL, QUERY_HEADS * HEAD_SIZE // UCOL, FF // UCOL]
    factors = [D ** (-0.5), INNER_WIDTH ** (-0.5), 4.0 * (QUERY_HEADS * HEAD_SIZE) ** (-0.5), 1.5 * FF ** (-0.5)]
    table = np.concatenate([np.full((count,), factor, np.float32) for count, factor in zip(counts, factors)])
    scales = jnp.asarray(table)[:, None, None]
    base = jax.random.truncated_normal(key, -4.0, 4.0, (UNITS, D, UCOL), jnp.float32)
    return (base * scales).astype(jnp.bfloat16)


def draw_small(key, part):
    key = jax.random.fold_in(key, 23)
    key_rows = jax.random.split(key, 7)
    gains = 1.0 + 0.1 * jax.random.truncated_normal(key_rows[0], -4.0, 4.0, (2 * D + INNER_WIDTH,), jnp.float32)
    taps = 0.5 * jax.random.truncated_normal(key_rows[1], -4.0, 4.0, (KW * CONV_CHANNELS,), jnp.float32)
    conv_bias = 0.2 * jax.random.truncated_normal(key_rows[2], -4.0, 4.0, (CONV_CHANNELS,), jnp.float32)
    base_step = jnp.exp(jax.random.uniform(key_rows[3], (HM,), jnp.float32, np.log(0.0017), np.log(0.0068)))
    dt_bias = jnp.log(jnp.expm1(base_step))
    a_log = jax.random.uniform(key_rows[4], (HM,), jnp.float32, np.log(60.0 / LEN), np.log(3.0))
    skip = jax.random.uniform(key_rows[5], (HM,), jnp.float32, 0.5, 1.5)
    dt_proj = 1.5 * D ** (-0.5) * jax.random.truncated_normal(key_rows[6], -4.0, 4.0, (D * HM,), jnp.float32)
    return jnp.concatenate([gains, taps, conv_bias, dt_bias, a_log, skip, dt_proj])


def block_levels(key, extent, cuts, least, top_value):
    def one(axis_at, shards_of):
        draws = jax.random.uniform(jax.random.fold_in(jax.random.fold_in(key, 6), axis_at), (shards_of,), jnp.float32, least / len(cuts), top_value / len(cuts))
        return jnp.repeat(jnp.exp(draws), extent[axis_at] // shards_of).reshape((-1,) + (1,) * (len(extent) - axis_at - 1))

    loudness = one(*cuts[0])
    for cut in cuts[1:]:
        loudness = loudness * one(*cut)
    return loudness


def noise(rng, dims, deviation, bound, shards=(), kind=jnp.bfloat16):
    factor_of = block_levels(rng, dims, shards, -0.22, 0.18) if shards else 1.0
    entries = jax.random.normal(rng, dims, jnp.float32) * deviation * factor_of
    return jnp.minimum(jnp.maximum(entries, -bound), bound).astype(kind)


def setup_inputs(seed: int = 0) -> dict:
    key_list = jax.random.split(jax.random.key(seed), 7)
    return {
        "hidden_in": noise(key_list[0], (NSEQ, LEN, D), 1.0, 6.0, ((0, 16), (1, 8)), jnp.float32),
        "cotangent": noise(key_list[1], (NSEQ, LEN, D), 1.0, 6.0, ((0, 16), (1, 8)), jnp.float32),
        "units": draw_units(jax.random.fold_in(key_list[6], 71), 0),
        "unit_momentum": noise(key_list[3], (UNITS, D, UCOL), (0.3 * TOKENS ** 0.5), 230.4, ((0, 8),), jnp.float32),
        "small": draw_small(jax.random.fold_in(key_list[6], 71), 0),
        "small_momentum": noise(key_list[5], (SMALL,), (0.3 * TOKENS ** 0.5), 230.4, (), jnp.float32),
    }


@jax.custom_vjp
def low(v):
    return lax.optimization_barrier(v.astype(jnp.bfloat16)).astype(jnp.float32)

@jax.custom_vjp
def low_back(v):
    return v

def low_keep(v):
    return (low(v), None)

def low_pass(kept, grad):
    return (grad,)

def back_keep(v):
    return (v, None)

def back_low(kept, grad):
    return (low(grad),)
low.defvjp(low_keep, low_pass)
low_back.defvjp(back_keep, back_low)
EPS = 1e-05
ROPE_BASE = 100000000000.0
NS_FIRST = 3.4445
NS_SECOND = -4.775
NS_THIRD = 2.0315
MOM_MAT = 0.95
MOM_VEC = 0.9
RATE_MAT = 0.6
DECAY_MAT = 0.1
RATE_VEC = 0.5
HIGHEST_PRECISION = lax.Precision.HIGHEST

def rms_norm(value_rows, gain):
    return value_rows * lax.rsqrt(lax.optimization_barrier(jnp.mean(value_rows * value_rows, axis=-1, keepdims=True)) + EPS) * gain

def sigmoid_linear(value_rows):
    return value_rows * jax.nn.sigmoid(value_rows)

def rope_tables(position):
    half = HEAD_SIZE // 2
    exponent = jnp.arange(half, dtype=jnp.float32) * (2.0 / HEAD_SIZE)
    frequency = jnp.power(ROPE_BASE, -exponent)
    angle = position.astype(jnp.float32)[:, None] * frequency[None, :]
    return (jnp.cos(angle), jnp.sin(angle))

def apply_rotary(value_rows, cosine_table, sine_table):
    half = value_rows.shape[-1] // 2
    front = value_rows[..., :half]
    behind = value_rows[..., half:]
    cos_b = cosine_table[:, None, :]
    sin_b = sine_table[:, None, :]
    return jnp.concatenate([front * cos_b - behind * sin_b, behind * cos_b + front * sin_b], axis=-1)

def split_small(small):
    widths = [D, D, INNER_WIDTH, KW * CONV_CHANNELS, CONV_CHANNELS, HM, HM, HM, D * HM]
    pieces = []
    offset = 0
    for count in widths:
        pieces.append(small[offset:offset + count])
        offset = offset + count
    pieces[3] = pieces[3].reshape(KW, CONV_CHANNELS)
    pieces[8] = pieces[8].reshape(D, HM)
    return tuple(pieces)

def orthogonalize(momentum):
    matrix = momentum.T / (jnp.sqrt(jnp.sum(momentum * momentum)) + 1e-07)
    for turn in range(5):
        square = jnp.dot(matrix, matrix.T, precision=HIGHEST_PRECISION)
        mixing = NS_SECOND * square + NS_THIRD * jnp.dot(square, square, precision=HIGHEST_PRECISION)
        matrix = NS_FIRST * matrix + jnp.dot(mixing, matrix, precision=HIGHEST_PRECISION)
    return matrix.T

def layer_sequence(hidden, weights, small):
    gain_in, gain_mid, gain_mixer, taps, conv_bias, dt_bias, a_log, skip_gain, dt_proj = split_small(small)
    sequence_length = hidden.shape[0]
    first_end = MIX_IN // UCOL
    second_end = first_end + 2 * FF // UCOL
    mamba_end = second_end + INNER_WIDTH // UCOL
    attn_end = mamba_end + QUERY_HEADS * HEAD_SIZE // UCOL
    position = jnp.arange(sequence_length, dtype=jnp.int32)
    cosine_table, sine_table = rope_tables(position)
    first = low(rms_norm(hidden, gain_in))
    projected_input = jnp.einsum('td,udc->tuc', first, weights[:first_end], precision=HIGHEST_PRECISION)
    projected_input = low_back(projected_input.reshape(sequence_length, MIX_IN))
    dt_raw = low_back(jnp.dot(first, low(dt_proj), precision=HIGHEST_PRECISION))
    gate_z = projected_input[:, :INNER_WIDTH]
    conv_in = projected_input[:, INNER_WIDTH:INNER_WIDTH + CONV_CHANNELS]
    query_pre = projected_input[:, INNER_WIDTH + CONV_CHANNELS:INNER_WIDTH + CONV_CHANNELS + QUERY_HEADS * HEAD_SIZE].reshape(sequence_length, QUERY_HEADS, HEAD_SIZE)
    prerotation_key = projected_input[:, INNER_WIDTH + CONV_CHANNELS + QUERY_HEADS * HEAD_SIZE:INNER_WIDTH + CONV_CHANNELS + (QUERY_HEADS + KEY_VALUE_HEADS) * HEAD_SIZE].reshape(sequence_length, KEY_VALUE_HEADS, HEAD_SIZE)
    preexpand_value = projected_input[:, INNER_WIDTH + CONV_CHANNELS + (QUERY_HEADS + KEY_VALUE_HEADS) * HEAD_SIZE:].reshape(sequence_length, KEY_VALUE_HEADS, HEAD_SIZE)
    padded = jnp.concatenate([jnp.zeros((KW - 1, CONV_CHANNELS), jnp.float32), conv_in], axis=0)
    convolved = conv_bias + taps[0] * padded[0:sequence_length]
    for tap in range(1, KW):
        convolved = convolved + taps[tap] * padded[tap:tap + sequence_length]
    active = sigmoid_linear(convolved)
    inputs = low(active[:, :INNER_WIDTH]).reshape(sequence_length, HM, HP)
    bmat = low(active[:, INNER_WIDTH:INNER_WIDTH + DS])
    cmat = low(active[:, INNER_WIDTH + DS:])
    step = jax.nn.softplus(dt_raw + dt_bias)
    logdecay = step * -jnp.exp(a_log)
    blocks = sequence_length // SPAN

    def span_step(state, pieces):
        block_in, block_b, block_c, block_step, block_log = pieces
        cumulative = jnp.cumsum(block_log, axis=0)
        size = block_log.shape[0]
        lower = (jnp.arange(size)[:, None] >= jnp.arange(size)[None, :])[:, :, None]
        gap = cumulative[:, None, :] - cumulative[None, :, :]
        fading = jnp.where(lower, jnp.exp(jnp.where(lower, gap, 0.0)), 0.0)
        correlation = jnp.dot(block_c, block_b.T, precision=HIGHEST_PRECISION)
        kernel = low(fading * correlation[:, :, None] * block_step[None, :, :])
        inside = jnp.einsum('tjh,jhp->thp', kernel, block_in, precision=HIGHEST_PRECISION)
        across = jnp.exp(cumulative)[:, :, None] * jnp.einsum('tn,hpn->thp', block_c, state, precision=HIGHEST_PRECISION)
        tail = jnp.exp(cumulative[-1][None, :] - cumulative) * block_step
        contrib = jnp.einsum('jh,jhp,jn->hpn', tail, block_in, block_b, precision=HIGHEST_PRECISION)
        new_state = jnp.exp(cumulative[-1])[:, None, None] * state + contrib
        return (new_state, inside + across + skip_gain[None, :, None] * block_in)
    start = jnp.zeros((HM, HP, DS), jnp.float32)
    final_state, mixed = lax.scan(jax.checkpoint(span_step), start, (inputs.reshape(blocks, SPAN, HM, HP), bmat.reshape(blocks, SPAN, DS), cmat.reshape(blocks, SPAN, DS), step.reshape(blocks, SPAN, HM), logdecay.reshape(blocks, SPAN, HM)))
    gated = mixed.reshape(sequence_length, INNER_WIDTH) * sigmoid_linear(gate_z)
    mixer_low = low(rms_norm(gated, gain_mixer))
    mamba_out = low_back(jnp.einsum('tuc,udc->td', mixer_low.reshape(sequence_length, INNER_WIDTH // UCOL, UCOL), weights[second_end:mamba_end], precision=HIGHEST_PRECISION))
    query_rows = low(apply_rotary(query_pre, cosine_table, sine_table))
    key_rows = low(apply_rotary(prerotation_key, cosine_table, sine_table))
    value_rows = low(preexpand_value)
    grouped_heads = query_rows.reshape(sequence_length, KEY_VALUE_HEADS, QUERY_HEADS // KEY_VALUE_HEADS, HEAD_SIZE)
    scores = jnp.einsum('tgrd,jgd->grtj', grouped_heads, key_rows, precision=HIGHEST_PRECISION) * HEAD_SIZE ** (-0.5)
    scores = low_back(scores)
    causal = position[None, :] <= position[:, None]
    masked = jnp.where(causal, scores, -1e+30)
    peak = lax.optimization_barrier(jnp.max(masked, axis=-1, keepdims=True))
    expo = jnp.exp(masked - peak)
    probs = expo / lax.optimization_barrier(jnp.sum(expo, axis=-1, keepdims=True))
    attended = jnp.einsum('grtj,jgd->tgrd', low(probs), value_rows, precision=HIGHEST_PRECISION)
    attended = low(low_back(attended.reshape(sequence_length, QUERY_HEADS * HEAD_SIZE)))
    attn_out = low_back(jnp.einsum('tuc,udc->td', attended.reshape(sequence_length, QUERY_HEADS * HEAD_SIZE // UCOL, UCOL), weights[mamba_end:attn_end], precision=HIGHEST_PRECISION))
    mid = hidden + mamba_out + attn_out
    second = low(rms_norm(mid, gain_mid))
    gate_up = jnp.einsum('td,udc->tuc', second, weights[first_end:second_end], precision=HIGHEST_PRECISION)
    gate_up = low_back(gate_up.reshape(sequence_length, 2 * FF))
    hidden_act = low(sigmoid_linear(gate_up[:, :FF]) * gate_up[:, FF:])
    mlp_out = low_back(jnp.einsum('tuc,udc->td', hidden_act.reshape(sequence_length, FF // UCOL, UCOL), weights[attn_end:], precision=HIGHEST_PRECISION))
    return mid + mlp_out

def reference(hidden_in, cotangent, units, unit_momentum, small, small_momentum):
    weights = units.astype(jnp.float32)

    def forward(inputs, weights, small):

        def one(carry, sequence):
            return (carry, jax.checkpoint(layer_sequence)(sequence, weights, small))
        carry, outputs = lax.scan(one, None, inputs)
        return outputs
    output, pull = jax.vjp(forward, hidden_in, weights, small)
    grad_input, grad_weights, grad_small = pull(cotangent)
    momentum_new = MOM_MAT * unit_momentum + grad_weights
    ortho = lax.map(orthogonalize, momentum_new)
    units_new = weights * (1.0 - RATE_MAT * DECAY_MAT) - RATE_MAT * ortho
    small_momentum_new = MOM_VEC * small_momentum + grad_small
    small_new = small - RATE_VEC / math.sqrt(TOKENS) * small_momentum_new
    return (output, grad_input, units_new, momentum_new, small_new, small_momentum_new)
```

```python
import math

import jax
import jax.numpy as jnp
from jax import lax
from jax.experimental import pallas as pl
from jax.experimental.pallas import tpu as pltpu
from jax.sharding import PartitionSpec as P

D = 1024
INNER_WIDTH = 1536
HM = 24
HP = 64
DS = 128
KW = 4
QUERY_HEADS = 8
KEY_VALUE_HEADS = 2
HEAD_SIZE = 64
FF = 2048
UCOL = 128
LEN = 1024
SEQS = 1
MIX_IN = 4096
CONV_CHANNELS = 1792


EPS = 1e-05
ROPE_BASE = 100000000000.0
NS_FIRST = 3.4445
NS_SECOND = -4.775
NS_THIRD = 2.0315
MOM_MAT = 0.95
MOM_VEC = 0.9
RATE_MAT = 0.6
DECAY_MAT = 0.1
RATE_VEC = 0.5
HIGHEST_PRECISION = lax.Precision.HIGHEST


MESH = pl.DeviceIdType.MESH
COLS = 96 * UCOL
SHARD = 12 * UCOL
PAGE = 2 * UCOL
PAGES = 48
SMALL_ROWS = 304
SMALL_HALF = SMALL_ROWS // 2
SMALL_SIZE = 37192
HEADS_ROW = 98
STEP_ROW = 104
AHEAD = 16
SLOTS = 12


def place():
    rep = lax.axis_index("rep")
    fsdp = lax.axis_index("fsdp")
    return (fsdp % 4, (rep // 8) * 2 + fsdp // 4, (rep // 2) % 4, rep % 2)


def device(x, y, z, c):
    return (((y // 2) * 4 + z) * 2 + c, (y % 2) * 4 + x)


def greet(others):
    barrier = pltpu.get_barrier_semaphore()
    for other in others:
        pl.semaphore_signal(barrier, inc=1, device_id=other, device_id_type=MESH)
    pl.semaphore_wait(barrier, len(others))


def push(source, target, send_sem, recv_sem, where):
    return pltpu.make_async_remote_copy(
        src_ref=source,
        dst_ref=target,
        send_sem=send_sem,
        recv_sem=recv_sem,
        device_id=where,
        device_id_type=MESH,
    )


def gather_kernel(
    units_ref,
    hidden_ref,
    cotangent_ref,
    gain_ref,
    out_ref,
    first_ref,
    low_ref,
    scale_ref,
    cosine_ref,
    sine_ref,
    held,
    earlier,
    hidden_held,
    cotangent_held,
    local_sem,
    out_sem,
    send_sem,
    recv_sem,
    core_send,
    core_recv,
    earlier_sem,
    row_sem,
):
    x, y, z, c = place()
    yl = y % 2
    parity = z % 2
    x_up, x_down = (device((x + 1) % 4, y, z, c), device((x + 3) % 4, y, z, c))
    y_up, y_down = (device(x, (y + 1) % 4, z, c), device(x, (y + 3) % 4, z, c))
    z_up, z_down = (device(x, y, (z + 1) % 4, c), device(x, y, (z + 3) % 4, c))
    sibling = device(x, y, z, 1 - c)
    mine = yl * 4 + x
    locals_ = []
    for j in range(12):
        for half in range(2):
            copy = pltpu.make_async_copy(
                units_ref.at[j, pl.ds(half * (D // 2), D // 2)],
                held.at[mine, j // 6, j % 6 // 3, half, :, pl.ds(j % 3 * UCOL, UCOL)],
                local_sem.at[2 * j + half],
            )
            copy.start()
            locals_.append(copy)
    rep, rank = (lax.axis_index("rep"), lax.axis_index("fsdp"))
    after, ahead = ((rep, (rank + 1) % 8), (rep, (rank + 7) % 8))
    greet([x_up, x_down, y_up, y_down, z_up, z_down, sibling, after, ahead])
    tokens = hidden_ref.shape[0]
    hidden_in = pltpu.make_async_copy(hidden_ref, hidden_held, row_sem.at[0])
    hidden_in.start()
    cotangent_in = pltpu.make_async_copy(cotangent_ref, cotangent_held, row_sem.at[1])
    cotangent_in.start()
    rows_on = push(
        hidden_ref.at[pl.ds(tokens - 8, 8)], earlier, earlier_sem.at[0], earlier_sem.at[1], after
    )
    rows_on.start()
    for copy in locals_:
        copy.wait()

    quarter = D // 4

    def chunk(offset, row, other, half, core, sub=None):
        shard = (yl + row) % 2 * 4 + (x + offset) % 4
        whole = held.at[shard, core, (parity + other) % 2, half]
        return whole if sub is None else whole.at[pl.ds(sub * quarter, quarter)]

    written = []

    def write(offset, row, other, half, core, sub=None):
        shard = (yl + row) % 2 * 4 + (x + offset) % 4
        part = (parity + other) % 2
        column = pl.multiple_of(shard * SHARD + core * (SHARD // 2) + part * (SHARD // 4), UCOL)
        first, count = (half * (D // 2), D // 2)
        if sub is not None:
            first, count = (first + sub * quarter, quarter)
        copy = pltpu.make_async_copy(
            chunk(offset, row, other, half, core, sub),
            out_ref.at[pl.ds(first, count), pl.ds(column, SHARD // 4)],
            out_sem.at[len(written)],
        )
        copy.start()
        written.append(copy)

    steps = (0, 3, 1, 2)
    arrivals = {}
    for q in range(2):
        arrivals[q] = (3, 0, q, 0)
        arrivals[2 + q] = (3, 0, q, 1)
        arrivals[4 + q] = (1, 0, q, 1)
        arrivals[6 + q] = (1, 0, q, 0)
        arrivals[8 + q] = (2, 0, q, 0)
        arrivals[10 + q] = (2, 0, q, 1)
    for i in range(4):
        for half in range(2):
            arrivals[12 + 2 * i + half] = (steps[i], 1, 0, half)
            arrivals[20 + 2 * i + half] = (steps[i], 1, 1, half)
    subs = {9: 0, 11: 0, 28: 1, 29: 1}
    arrivals[28] = (2, 0, 1, 0)
    arrivals[29] = (2, 0, 1, 1)
    sent = []

    def send(piece, index, where):
        view = chunk(*piece, c, subs.get(index))
        copy = push(view, view, send_sem.at[len(sent)], recv_sem.at[index], where)
        copy.start()
        sent.append(copy)

    def own(q, half, index, where):
        send((0, 0, q, half), index, where)

    own(0, 0, 0, x_up)
    own(0, 1, 4, x_down)
    own(0, 0, 12, y_up)
    own(0, 1, 13, y_down)
    own(0, 1, 2, x_up)
    own(0, 0, 6, x_down)
    forwards = {
        0: [(8, x_up), (14, y_up)],
        4: [(10, x_down), (17, y_down)],
        12: [(20, z_up)],
        13: [(21, z_down)],
        2: [(15, y_down)],
        6: [(16, y_up)],
        14: [(22, z_up)],
        17: [(25, z_down)],
        8: [(18, y_up), (28, z_up)],
        10: [(19, y_down), (29, z_down)],
        15: [(23, z_down)],
        16: [(24, z_up)],
        1: [(9, x_up)],
        5: [(11, x_down)],
        18: [(26, z_up)],
        19: [(27, z_down)],
    }
    late = {2: (1, 0, 1, x_up), 6: (1, 1, 5, x_down), 8: (1, 1, 3, x_up), 10: (1, 0, 7, x_down)}
    sequence = (0, 4, 12, 13, 2, 6, 14, 17, 20, 21, 8, 10, 15, 16, 22, 25)
    sequence = sequence + (1, 5, 18, 19, 23, 24, 28, 29, 3, 7, 26, 27, 9, 11)
    for core in (c, 1 - c):
        for q in range(2):
            for half in range(2):
                write(0, 0, q, half, core)

    def normal(value):
        scale = lax.rsqrt(jnp.mean(value * value, axis=1, keepdims=True) + EPS)
        return (scale, (value * scale * gain_ref[...]).astype(jnp.bfloat16))

    position = lax.broadcasted_iota(jnp.int32, (tokens, 128), 0) + rank * tokens
    lane = lax.broadcasted_iota(jnp.int32, (tokens, 128), 1)
    half = HEAD_SIZE // 2
    exponent = (lane % half).astype(jnp.float32) * (-2.0 * math.log(ROPE_BASE) / HEAD_SIZE)
    angle = position.astype(jnp.float32) * jnp.exp(exponent)
    cosine_ref[...] = jnp.cos(angle)
    sine = jnp.sin(angle)
    sine_ref[...] = jnp.where(lane % HEAD_SIZE < half, -sine, sine)
    hidden_in.wait()
    cotangent_in.wait()
    scale, first = normal(hidden_held[...])
    scale_ref[...] = jnp.broadcast_to(scale, scale_ref.shape)
    first_ref[AHEAD : AHEAD + tokens] = first
    low_ref[...] = cotangent_held[...].astype(jnp.bfloat16)
    rows_on.wait_recv()
    before = jnp.where(rank > 0, earlier[...], 0.0)
    _, before = normal(jnp.concatenate([jnp.zeros_like(before), before]))
    first_ref[0:AHEAD] = before
    crossing = []

    def land(index):
        view = chunk(*arrivals[index], 1 - c, subs.get(index))
        push(view, view, core_send.at[index], core_recv.at[index], sibling).wait_recv()
        write(*arrivals[index], 1 - c, subs.get(index))

    lag = 8
    for number, index in enumerate(sequence):
        view = chunk(*arrivals[index], c, subs.get(index))
        push(view, view, send_sem.at[0], recv_sem.at[index], sibling).wait_recv()
        for target, where in forwards.get(index, ()):
            send(arrivals[index], target, where)
        if index in late:
            own(*late[index])
        copy = push(view, view, core_send.at[index], core_recv.at[index], sibling)
        copy.start()
        crossing.append(copy)
        write(*arrivals[index], c, subs.get(index))
        if number >= lag:
            land(sequence[number - lag])
    for index in sequence[len(sequence) - lag :]:
        land(index)
    for copy in sent + crossing:
        copy.wait_send()
    for copy in written:
        copy.wait()
    rows_on.wait_send()


def gather_weights(units, hidden, cotangent, gain):
    vmem = pl.BlockSpec(memory_space=pltpu.VMEM)
    dma = pltpu.SemaphoreType.DMA
    tokens = hidden.shape[0]
    low = jnp.bfloat16
    return pl.pallas_call(
        gather_kernel,
        out_shape=(
            jax.ShapeDtypeStruct((D, COLS), low),
            jax.ShapeDtypeStruct((AHEAD + tokens, D), low),
            jax.ShapeDtypeStruct((tokens, D), low),
            jax.ShapeDtypeStruct((tokens, 128), jnp.float32),
            jax.ShapeDtypeStruct((tokens, 128), jnp.float32),
            jax.ShapeDtypeStruct((tokens, 128), jnp.float32),
        ),
        in_specs=[pl.BlockSpec(memory_space=pltpu.HBM)] * 3 + [vmem],
        out_specs=(pl.BlockSpec(memory_space=pl.ANY), vmem, vmem, vmem, vmem, vmem),
        scratch_shapes=[
            pltpu.VMEM((8, 2, 2, 2, D // 2, SHARD // 4), low),
            pltpu.VMEM((8, D), jnp.float32),
            pltpu.VMEM((tokens, D), jnp.float32),
            pltpu.VMEM((tokens, D), jnp.float32),
            dma((24,)),
            dma((68,)),
            dma((30,)),
            dma((30,)),
            dma((30,)),
            dma((30,)),
            dma((2,)),
            dma((2,)),
        ],
        compiler_params=pltpu.CompilerParams(
            collective_id=0, has_side_effects=True, vmem_limit_bytes=60 * 1024 * 1024
        ),
        name="gather_weights",
    )(units, hidden, cotangent, gain)


def reduce_kernel(
    first_ref,
    second_ref,
    mid_ref,
    last_ref,
    columns_ref,
    small_ref,
    own_ref,
    small_out,
    turned,
    stage,
    total,
    sibling_half,
    ring_a,
    ring_b,
    ring_c,
    ring_second,
    ring_third,
    small_core,
    small_x,
    small_y,
    small_z,
    core_send,
    core_recv,
    ring_send,
    ring_recv,
    own_send,
    own_recv,
    cross_send,
    cross_recv,
    small_send,
    small_recv,
):
    x, y, z, c = place()
    yl, yh = (y % 2, y // 2)
    sibling = device(x, y, z, 1 - c)

    def along(axis, step):
        if axis == 0:
            return device((x + step) % 4, y, z, c)
        if axis == 1:
            return device(x, (y + step) % 4, z, c)
        return device(x, y, (z + step) % 4, c)

    greet([sibling] + [along(axis, step) for axis in range(3) for step in (1, 2, 3)])

    turned[0] = first_ref[AHEAD:].T
    turned[1] = second_ref[...].T
    small_cross = push(
        small_ref.at[1 - c], small_core, small_send.at[0], small_recv.at[0], sibling
    )
    small_cross.start()
    groups = (
        (2, lambda i: (0, i)),
        (1, lambda i: (i % 2, i // 2)),
        (0, lambda i: (0, (x + 2 + 3 * i) % 4)),
        (2, lambda i: (1, i)),
        (1, lambda i: (i % 2, 2 + i // 2)),
        (0, lambda i: (1, (x + 2 + 3 * i) % 4)),
    )

    def gradient(k, s, core):
        page = s * 6 + k * 2 + core
        return jnp.dot(
            turned[page // 16 + page // 40],
            columns_ref[:, pl.ds(pl.multiple_of(page * PAGE, PAGE), PAGE)],
            preferred_element_type=jnp.float32,
        ).reshape(4, 2, 128, PAGE)

    def crossing(slot, k, row, column, number):
        return push(
            stage.at[slot],
            sibling_half.at[k, row, column],
            core_send.at[number],
            core_recv.at[number],
            sibling,
        )

    def hand_over(group):
        k, where = groups[group]
        start = 4 * group

        def give(i, carry):
            number = start + i
            row, column = where(i)
            slot = number
            if start >= SLOTS:
                slot = number - SLOTS
                crossing(slot, k, row, column, slot).wait_send()
            stage[slot] = gradient(k, row * 4 + column, 1 - c).astype(jnp.bfloat16)
            crossing(slot, k, row, column, number).start()
            return carry

        lax.fori_loop(0, 4, give, 0)

    def core_sum(group):
        k, where = groups[group]
        start = 4 * group

        def take(i, carry):
            number = start + i
            row, column = where(i)
            slot = number if start < SLOTS else number - SLOTS
            crossing(slot, k, row, column, number).wait_recv()
            value = gradient(k, row * 4 + column, c)
            value = value + sibling_half[k, row, column].astype(jnp.float32)
            total[k, row, column] = value.astype(jnp.bfloat16)
            return carry

        lax.fori_loop(0, 4, take, 0)

    position = (x, y, z)

    def view(k, phase, part, at, half):
        if phase == 0:
            if k == 0:
                return total.at[0, part, at, pl.ds(2 * half, 2)]
            if k == 1:
                return total.at[1, at % 2, 2 * part + half, :, at // 2]
            return total.at[2, part, pl.ds(2 * half, 2), at]
        if phase == 1:
            if k == 0:
                return total.at[0, at % 2, x, pl.ds(2 * half, 2), at // 2]
            if k == 1:
                return total.at[1, yl, pl.ds(2 * half, 2), at, yh]
            return total.at[2, half, at, z]
        rows = pl.ds(64 * half, 64)
        if k == 0:
            return total.at[0, yl, x, at, yh, rows]
        if k == 1:
            return total.at[1, yl, at, z, yh, rows]
        return total.at[2, at % 2, x, z, at // 2, rows]

    def slot(k, phase, part, index):
        if phase == 0:
            return (ring_a, ring_b, ring_c)[k].at[part, index]
        return (ring_second, ring_third)[phase - 1].at[k, index]

    ring_copies = {}

    def ring_push(k, phase, part, at, half, index, step):
        number = ((2 * k + part) if phase == 0 else 3 + 3 * phase + k) * 6 + index
        copy = push(
            view(k, phase, part, at, half),
            slot(k, phase, part, index),
            ring_send.at[number],
            ring_recv.at[number],
            along((k + phase) % 3, step),
        )
        copy.start()
        ring_copies[k, phase, part, index] = copy

    def blocks(ref):
        shape = ref.shape
        if len(shape) == 4:
            return [(a, b) for a in range(shape[0]) for b in range(shape[1])]
        if len(shape) == 3:
            return [(a,) for a in range(shape[0])]
        return [()]

    def accumulate(goal, parts):
        shape = goal.shape
        lead = len(shape) - 2
        if lead == 0:
            value = goal[...].astype(jnp.float32)
            for part in parts:
                value = value + part[...].astype(jnp.float32)
            goal[...] = value.astype(jnp.bfloat16)
            return

        def one(i, carry):
            index = (i,) if lead == 1 else (i // shape[1], i % shape[1])
            value = goal[index].astype(jnp.float32)
            for part in parts:
                value = value + part[index].astype(jnp.float32)
            goal[index] = value.astype(jnp.bfloat16)
            return carry

        lax.fori_loop(0, math.prod(shape[:lead]), one, 0)

    def ring_start(k, phase, part=0):
        me = position[(k + phase) % 3]
        ring_push(k, phase, part, (me + 2) % 4, 0, 0, 1)
        ring_push(k, phase, part, (me + 2) % 4, 1, 1, 3)
        ring_push(k, phase, part, (me + 1) % 4, 1, 2, 1)
        ring_push(k, phase, part, (me + 3) % 4, 0, 4, 3)

    def ring_relay(k, phase, part=0):
        me = position[(k + phase) % 3]
        ring_copies[k, phase, part, 0].wait_recv()
        accumulate(view(k, phase, part, (me + 1) % 4, 0), [slot(k, phase, part, 0)])
        ring_push(k, phase, part, (me + 1) % 4, 0, 3, 1)
        ring_copies[k, phase, part, 1].wait_recv()
        accumulate(view(k, phase, part, (me + 3) % 4, 1), [slot(k, phase, part, 1)])
        ring_push(k, phase, part, (me + 3) % 4, 1, 5, 3)

    def ring_finish(k, phase, part=0):
        me = position[(k + phase) % 3]
        for index in (2, 4, 3, 5):
            ring_copies[k, phase, part, index].wait_recv()
        for half, first, second in ((1, 2, 5), (0, 3, 4)):
            accumulate(
                view(k, phase, part, me, half),
                [slot(k, phase, part, first), slot(k, phase, part, second)],
            )

    small_copies = []

    def small_spread(buffer, me, axis):
        group = []
        for step in (1, 3, 2):
            number = 1 + axis * 3 + (0, 0, 2, 1)[step]
            copy = push(
                buffer.at[me],
                buffer.at[me],
                small_send.at[number],
                small_recv.at[number],
                along(axis, step),
            )
            copy.start()
            group.append((copy, step, number))
        small_copies.extend(group)
        return group

    def small_sum(buffer, me, group):
        for _, step, number in group:
            came = buffer.at[(me + 4 - step) % 4]
            push(came, came, small_send.at[number], small_recv.at[number], sibling).wait_recv()
        return (buffer[0] + buffer[1]) + (buffer[2] + buffer[3])

    hand_over(0)
    turned[2] = mid_ref[...].T
    turned[3] = last_ref[...].T
    hand_over(1)
    core_sum(0)
    ring_start(2, 0, 0)
    hand_over(2)
    core_sum(1)
    ring_start(1, 0, 0)
    hand_over(3)
    core_sum(2)
    ring_start(0, 0, 0)
    ring_relay(2, 0, 0)
    hand_over(4)
    core_sum(3)
    ring_start(2, 0, 1)
    ring_relay(1, 0, 0)
    small_cross.wait_recv()
    small_x[x] = small_ref[c] + small_core[...]
    spread = small_spread(small_x, x, 0)
    hand_over(5)
    core_sum(4)
    ring_start(1, 0, 1)
    ring_relay(0, 0, 0)
    ring_finish(2, 0, 0)
    core_sum(5)
    ring_start(0, 0, 1)
    ring_relay(2, 0, 1)
    ring_finish(1, 0, 0)
    small_y[y] = small_sum(small_x, x, spread)
    spread = small_spread(small_y, y, 1)
    ring_relay(1, 0, 1)
    ring_finish(2, 0, 1)
    ring_start(2, 1)
    ring_finish(0, 0, 0)
    ring_relay(0, 0, 1)
    ring_finish(1, 0, 1)
    ring_start(1, 1)
    ring_relay(2, 1)
    ring_finish(0, 0, 1)
    ring_start(0, 1)
    small_z[z] = small_sum(small_y, y, spread)
    spread = small_spread(small_z, z, 2)
    ring_relay(1, 1)
    ring_finish(2, 1)
    ring_start(2, 2)
    ring_relay(0, 1)
    ring_finish(1, 1)
    ring_start(1, 2)
    ring_relay(2, 2)
    ring_finish(0, 1)
    ring_start(0, 2)
    small_out[c] = small_sum(small_z, z, spread)
    small_back = push(
        small_out.at[c], small_out.at[c], small_send.at[10], small_recv.at[10], sibling
    )
    small_back.start()
    ring_relay(1, 2)
    far = along(1, 2)
    up, down = (along(2, 1), along(2, 3))
    below, above, opposite = ((z + 3) % 4, (z + 1) % 4, (z + 2) % 4)
    strips = []
    crossed = []

    def strip(k, core, zz, yy):
        return own_ref.at[k, core, :, zz, yy]

    def give_strip(k, zz, yy, index, where):
        view = strip(k, c, zz, yy)
        copy = push(view, view, own_send.at[7 * k + index], own_recv.at[7 * k + index], where)
        copy.start()
        strips.append(copy)

    def cross_strip(k, zz, yy):
        number = len(crossed)
        view = strip(k, c, zz, yy)
        copy = push(view, view, cross_send.at[number], cross_recv.at[number], sibling)
        copy.start()
        crossed.append((copy, k, zz, yy))

    def take_strip(k, zz, yy, index):
        view = strip(k, c, zz, yy)
        push(view, view, own_send.at[7 * k + index], own_recv.at[7 * k + index], far).wait_recv()
        cross_strip(k, zz, yy)

    def spread_first(k):
        ring_finish(k, 2)
        summed = total[k, yl, x, z, yh]
        for unit in range(2):
            own_ref[k, c, unit, z, yh] = summed[:, unit * UCOL : (unit + 1) * UCOL]
        give_strip(k, z, yh, 0, far)
        give_strip(k, z, yh, 1, up)
        give_strip(k, z, yh, 2, down)
        cross_strip(k, z, yh)

    def spread_second(k):
        take_strip(k, z, 1 - yh, 0)
        give_strip(k, z, 1 - yh, 3, up)
        give_strip(k, z, 1 - yh, 4, down)

    def spread_third(k):
        take_strip(k, below, yh, 1)
        give_strip(k, below, yh, 5, up)
        take_strip(k, above, yh, 2)
        take_strip(k, above, 1 - yh, 4)
        give_strip(k, above, 1 - yh, 6, down)
        take_strip(k, below, 1 - yh, 3)

    def spread_last(k):
        take_strip(k, opposite, yh, 5)
        take_strip(k, opposite, 1 - yh, 6)

    spread_first(2)
    ring_relay(0, 2)
    spread_first(1)
    spread_second(2)
    spread_first(0)
    spread_second(1)
    spread_third(2)
    spread_second(0)
    spread_third(1)
    spread_last(2)
    spread_third(0)
    spread_last(1)
    spread_last(0)
    for copy in strips:
        copy.wait_send()
    for number, (copy, k, zz, yy) in enumerate(crossed):
        copy.wait_send()
        view = strip(k, 1 - c, zz, yy)
        push(view, view, cross_send.at[number], cross_recv.at[number], sibling).wait_recv()
    for copy in ring_copies.values():
        copy.wait_send()
    for number in range(24 - SLOTS, 24):
        crossing(number % SLOTS, 0, 0, 0, number).wait_send()
    for copy, _, _ in small_copies:
        copy.wait_send()
    small_cross.wait_send()
    small_back.wait_send()
    back = small_out.at[1 - c]
    push(back, back, small_send.at[10], small_recv.at[10], sibling).wait_recv()


def reduce_gradients(first, second, mid, last, columns, small):
    vmem = pl.BlockSpec(memory_space=pltpu.VMEM)
    dma = pltpu.SemaphoreType.DMA
    low = jnp.bfloat16
    tokens = second.shape[0]
    return pl.pallas_call(
        reduce_kernel,
        out_shape=(
            jax.ShapeDtypeStruct((3, 2, 2, 4, 2, 128, UCOL), low),
            jax.ShapeDtypeStruct((2, SMALL_HALF, 128), jnp.float32),
        ),
        in_specs=[vmem] * 6,
        out_specs=(vmem, vmem),
        scratch_shapes=[
            pltpu.VMEM((4, D, tokens), low),
            pltpu.VMEM((SLOTS, 4, 2, 128, PAGE), low),
            pltpu.VMEM((3, 2, 4, 4, 2, 128, PAGE), low),
            pltpu.VMEM((3, 2, 4, 4, 2, 128, PAGE), low),
            pltpu.VMEM((2, 6, 2, 2, 128, PAGE), low),
            pltpu.VMEM((2, 6, 4, 128, PAGE), low),
            pltpu.VMEM((2, 6, 2, 2, 128, PAGE), low),
            pltpu.VMEM((3, 6, 2, 128, PAGE), low),
            pltpu.VMEM((3, 6, 64, PAGE), low),
            pltpu.VMEM((SMALL_HALF, 128), jnp.float32),
            pltpu.VMEM((4, SMALL_HALF, 128), jnp.float32),
            pltpu.VMEM((4, SMALL_HALF, 128), jnp.float32),
            pltpu.VMEM((4, SMALL_HALF, 128), jnp.float32),
            dma((24,)),
            dma((24,)),
            dma((72,)),
            dma((72,)),
            dma((21,)),
            dma((21,)),
            dma((24,)),
            dma((24,)),
            dma((11,)),
            dma((11,)),
        ],
        compiler_params=pltpu.CompilerParams(
            collective_id=1, has_side_effects=True, vmem_limit_bytes=58 * 1024 * 1024
        ),
        name="reduce_gradients",
    )(first, second, mid, last, columns, small)


def spread_kernel(own_ref, out_ref, send_sem, recv_sem, cross_send, cross_recv):
    x, y, z, c = place()
    sibling = device(x, y, z, 1 - c)
    up, down = (device(x, y, (z + 1) % 4, c), device(x, y, (z + 3) % 4, c))
    greet([sibling, up, down])
    half, quarter = (D // 2, D // 4)
    for unit in range(2):
        for part in range(2):
            piece = own_ref[unit, part * half : (part + 1) * half]
            if unit == 0:
                out_ref[z, 4 * c + part] = piece
            else:

                @pl.when(c == part)
                def _():
                    out_ref[z, 2 + part] = piece

    def strip(zz, core, rows):
        return out_ref.at[zz, pl.ds(3 * core, 3), pl.ds(rows * quarter, quarter)]

    sent = []

    def send(zz, rows, number, where):
        view = strip(zz, c, rows)
        copy = push(view, view, send_sem.at[number], recv_sem.at[number], where)
        copy.start()
        sent.append(copy)

    crossed = []

    def cross(zz, rows):
        number = len(crossed)
        view = strip(zz, c, rows)
        copy = push(view, view, cross_send.at[number], cross_recv.at[number], sibling)
        copy.start()
        crossed.append((copy, zz, rows))

    def came(zz, rows, number):
        view = strip(zz, c, rows)
        push(view, view, send_sem.at[number], recv_sem.at[number], up).wait_recv()
        cross(zz, rows)

    below, above, opposite = ((z + 3) % 4, (z + 1) % 4, (z + 2) % 4)
    send(z, 0, 0, up)
    send(z, 1, 1, down)
    send(z, 1, 2, up)
    send(z, 0, 3, down)
    cross(z, 0)
    cross(z, 1)
    came(below, 0, 0)
    send(below, 0, 4, up)
    came(above, 1, 1)
    send(above, 1, 5, down)
    came(below, 1, 2)
    came(above, 0, 3)
    came(opposite, 0, 4)
    came(opposite, 1, 5)
    for copy in sent:
        copy.wait_send()
    for number, (copy, zz, rows) in enumerate(crossed):
        copy.wait_send()
        view = strip(zz, 1 - c, rows)
        push(view, view, cross_send.at[number], cross_recv.at[number], sibling).wait_recv()


def spread_blocks(own):
    vmem = pl.BlockSpec(memory_space=pltpu.VMEM)
    dma = pltpu.SemaphoreType.DMA
    return pl.pallas_call(
        spread_kernel,
        out_shape=jax.ShapeDtypeStruct((4, 6, D // 2, UCOL), own.dtype),
        in_specs=[vmem],
        out_specs=vmem,
        scratch_shapes=[dma((6,)), dma((6,)), dma((8,)), dma((8,))],
        compiler_params=pltpu.CompilerParams(
            collective_id=2, has_side_effects=True, vmem_limit_bytes=16 * 1024 * 1024
        ),
        name="spread_blocks",
    )(own)


def orthogonalize_kernel(index_ref, first_ref, second_ref, out_ref):
    def split(a):
        high = a.astype(jnp.bfloat16)
        return (high, (a - high.astype(jnp.float32)).astype(jnp.bfloat16))

    def exact(a, b, contract):
        def product(left, right):
            return lax.dot_general(
                left, right, (((1,), (contract,)), ((), ())), preferred_element_type=jnp.float32
            )

        return product(a[0], b[0]) + (product(a[0], b[1]) + product(a[1], b[0]))

    def start(ref):
        momentum = ref[0]
        return momentum.T / (jnp.sqrt(jnp.sum(momentum * momentum)) + 1e-07)

    matrices = [start(first_ref), start(second_ref)]
    for turn in range(5):
        parts = [split(matrix) for matrix in matrices]
        squares = [exact(part, part, 1) for part in parts]
        halves = [split(square) for square in squares]
        mixing = [
            NS_SECOND * square + NS_THIRD * exact(half, half, 0)
            for square, half in zip(squares, halves)
        ]
        matrices = [
            NS_FIRST * matrix + exact(split(mix), part, 0)
            for matrix, mix, part in zip(matrices, mixing, parts)
        ]
    for unit in range(2):
        out_ref[unit] = matrices[unit].T.astype(jnp.bfloat16)


def orthogonalize_two(momentum, index):
    return pl.pallas_call(
        orthogonalize_kernel,
        grid_spec=pltpu.PrefetchScalarGridSpec(
            num_scalar_prefetch=1,
            grid=(1,),
            in_specs=[
                pl.BlockSpec((1, D, UCOL), lambda i, index: (index[0], 0, 0)),
                pl.BlockSpec((1, D, UCOL), lambda i, index: (index[1], 0, 0)),
            ],
            out_specs=pl.BlockSpec((2, D, UCOL), lambda i, index: (0, 0, 0)),
        ),
        out_shape=jax.ShapeDtypeStruct((2, D, UCOL), jnp.bfloat16),
        compiler_params=pltpu.CompilerParams(vmem_limit_bytes=24 * 1024 * 1024),
        name="orthogonalize_two",
    )(index, momentum, momentum)


HEADS_WIDE = 128
KV_WIDTH = 2 * KEY_VALUE_HEADS * HEAD_SIZE
Q_WIDTH = QUERY_HEADS * HEAD_SIZE
F32 = jnp.float32
LOW = jnp.bfloat16


def mm(a, b, ca=1, cb=0, precision=None):
    return lax.dot_general(
        a, b, (((ca,), (cb,)), ((), ())), precision=precision, preferred_element_type=F32
    )


def head_map():
    head = lax.broadcasted_iota(jnp.int32, (HEADS_WIDE, INNER_WIDTH), 0)
    lane = lax.broadcasted_iota(jnp.int32, (HEADS_WIDE, INNER_WIDTH), 1)
    return (lane // HP == head).astype(F32)


def widen(values, heads):
    return mm(values, heads, precision=HIGHEST_PRECISION)


def per_head(values, heads):
    return mm(values, heads, 1, 1, precision=HIGHEST_PRECISION)


def swap_halves(value):
    width = value.shape[1]
    lane = lax.broadcasted_iota(jnp.int32, value.shape, 1)
    quarter = HEAD_SIZE // 2
    up = pltpu.roll(value, width - quarter, 1)
    down = pltpu.roll(value, quarter, 1)
    return jnp.where(lane % HEAD_SIZE < quarter, up, down)


def rotate(value, cosine, sine):
    parts = []
    swapped = swap_halves(value)
    for i in range(value.shape[1] // 128):
        lanes = slice(i * 128, (i + 1) * 128)
        parts.append(value[:, lanes] * cosine + swapped[:, lanes] * sine)
    return jnp.concatenate(parts, axis=1) if len(parts) > 1 else parts[0]


def rotary_part(proj_ref, cosine_ref, sine_ref, query_ref, kv_ref):
    cosine, sine = (cosine_ref[...], sine_ref[...])
    start = INNER_WIDTH + CONV_CHANNELS
    query = rotate(proj_ref[AHEAD:, start : start + Q_WIDTH], cosine, sine)
    query_ref[...] = query.astype(LOW)
    start = start + Q_WIDTH
    half = KV_WIDTH // 2
    kv_ref[:, :half] = rotate(proj_ref[AHEAD:, start : start + half], cosine, sine).astype(LOW)
    kv_ref[:, half:] = proj_ref[AHEAD:, start + half :].astype(LOW)


def convolve(extended, conv_in, halo, taps_ref, bias_ref):
    tokens = conv_in.shape[0]
    extended[0:8] = halo
    extended[8 : 8 + tokens] = conv_in
    total = bias_ref[...] + taps_ref[0:1] * extended[5 : 5 + tokens]
    for tap in range(1, KW):
        total = total + taps_ref[tap : tap + 1] * extended[5 + tap : 5 + tap + tokens]
    return total


def lower_ones(tokens):
    row = lax.broadcasted_iota(jnp.int32, (tokens, tokens), 0)
    column = lax.broadcasted_iota(jnp.int32, (tokens, tokens), 1)
    return (row >= column).astype(F32)


def softplus(value):
    return jnp.maximum(value, 0.0) + jnp.log1p(jnp.exp(-jnp.abs(value)))


def front_kernel(
    proj_ref,
    dt_ref,
    small_ref,
    cosine_ref,
    sine_ref,
    query_ref,
    kv_ref,
    xs_ref,
    bc_ref,
    cum_ref,
    step_ref,
    contrib_ref,
    decay_ref,
    taps_ref,
    bias_ref,
    heads_ref,
    gain_ref,
    extended,
):
    def wide_row(start, width):
        pieces = [small_ref[start + i : start + i + 1] for i in range(width // 128)]
        return jnp.concatenate(pieces, axis=1)

    gain_ref[...] = wide_row(2 * D // 128, INNER_WIDTH)
    start = (2 * D + INNER_WIDTH) // 128
    for tap in range(KW):
        taps_ref[tap : tap + 1] = wide_row(start + tap * CONV_CHANNELS // 128, CONV_CHANNELS)
    start = start + KW * CONV_CHANNELS // 128
    bias_ref[...] = wide_row(start, CONV_CHANNELS)
    start = start + CONV_CHANNELS // 128
    packed = jnp.broadcast_to(small_ref[start : start + 1], (8, HEADS_WIDE))
    row = lax.broadcasted_iota(jnp.int32, (8, HEADS_WIDE), 0)
    lane = lax.broadcasted_iota(jnp.int32, (8, HEADS_WIDE), 1)
    values = jnp.where(row == 1, pltpu.roll(packed, HEADS_WIDE - HM, 1), packed)
    values = jnp.where(row == 2, pltpu.roll(packed, HEADS_WIDE - 2 * HM, 1), values)
    heads_ref[...] = jnp.where((lane < HM) & (row < 3), values, 0.0)
    rotary_part(proj_ref, cosine_ref, sine_ref, query_ref, kv_ref)
    tokens = xs_ref.shape[0]
    channels = slice(INNER_WIDTH, INNER_WIDTH + CONV_CHANNELS)
    convolved = convolve(
        extended, proj_ref[AHEAD:, channels], proj_ref[AHEAD - 8 : AHEAD, channels], taps_ref, bias_ref
    )
    active = (convolved * jax.nn.sigmoid(convolved)).astype(LOW)
    xs = active[:, :INNER_WIDTH]
    xs_ref[...] = xs
    bc_ref[...] = active[:, INNER_WIDTH:]
    step = softplus(dt_ref[AHEAD:] + heads_ref[0:1])
    rate = -jnp.exp(heads_ref[1:2])
    cum = mm(lower_ones(tokens), step * rate, precision=HIGHEST_PRECISION)
    step_ref[...] = step
    cum_ref[...] = cum
    last = cum[tokens - 1 : tokens]
    tail = jnp.exp(last - cum) * step
    scaled = (xs.astype(F32) * widen(tail, head_map())).astype(LOW)
    contrib_ref[...] = mm(scaled, active[:, INNER_WIDTH : INNER_WIDTH + DS], 0, 0).astype(LOW)
    decay_ref[...] = jnp.broadcast_to(jnp.exp(last), decay_ref.shape)


def fading_of(cum, cum_rows, head, lower):
    gap = cum[:, head : head + 1] - cum_rows[head : head + 1]
    return jnp.where(lower, jnp.exp(jnp.where(lower, gap, 0.0)), 0.0)


CHUNK = INNER_WIDTH // 4


def exchange_kernel(direction, forward, *refs):
    extra_in, extra_out = (3, 2) if forward else (10, 5)
    own_ref, decay_ref, kv_ref = refs[:3]
    inputs = refs[3 : 3 + extra_in]
    out_ref, kv_out = refs[3 + extra_in : 5 + extra_in]
    outputs = refs[5 + extra_in : 5 + extra_in + extra_out]
    rest = refs[5 + extra_in + extra_out :]
    (
        got,
        total,
        arriving,
        decays,
        factors,
        kv_got,
        columns_ref,
        rows_ref,
        kv_grad,
        turned,
        held,
        held_sem,
        send_sem,
        recv_sem,
    ) = rest
    x, y, z, c = place()
    row = y % 2
    first_row = 0 if direction == 1 else 1
    along = x if direction == 1 else 3 - x
    up = device((x + 4 + direction) % 4, y, z, c)
    down = device((x + 4 - direction) % 4, y, z, c)
    opposite = device((x + 2) % 4, y, z, c)
    partner = device(x, y + 1 - 2 * row, z, c)
    greet([up, down, opposite, partner])
    sent = []

    def make(source, target, number, where):
        return push(source, target, send_sem.at[number], recv_sem.at[number], where)

    def send(source, target, number, where):
        copy = make(source, target, number, where)
        copy.start()
        sent.append(copy)

    def came(view, number):
        make(view, view, number, partner).wait_recv()

    def rows(chunk):
        return pl.ds(chunk * CHUNK, CHUNK)

    def spread(chunk, where, slot, number):
        send(own_ref.at[rows(chunk)], got.at[slot, rows(chunk)], number, where)

    def relay(chunk, slot, number, where):
        send(got.at[slot, rows(chunk)], got.at[1, rows(chunk)], number, where)

    send(decay_ref, decays.at[0], 0, up)
    send(decay_ref, decays.at[1], 1, opposite)
    send(decay_ref, decays.at[2], 2, down)
    if forward:
        for slot, number, where in ((1, 3, up), (2, 4, opposite), (3, 5, down)):
            send(kv_ref, kv_out.at[slot], number, where)
        kv_out[0] = kv_ref[...]

        @pl.when(row == 0)
        def _():
            kv_out[4:8] = jnp.zeros_like(kv_out[4:8])

        downs = stream(inputs[2], held, held_sem, COLS - FF)

    spread(0, up, 0, 7)
    spread(2, down, 2, 13)
    spread(2, up, 0, 9)
    spread(0, down, 2, 11)
    spread(1, up, 0, 8)
    spread(3, down, 2, 14)
    if forward:
        for slot in (1, 2, 3):
            came(kv_out.at[slot], 2 + slot)

        @pl.when(row == 0)
        def _():
            make(kv_out.at[0:4], kv_out.at[4:8], 6, partner).start()

    came(got.at[0, rows(0)], 7)
    relay(0, 0, 15, up)
    came(got.at[2, rows(2)], 13)
    relay(2, 2, 17, down)
    spread(3, up, 0, 10)
    spread(1, down, 2, 12)
    if not forward:
        attention_back_part(
            lax.axis_index("fsdp"), inputs[8], kv_ref, inputs[9], outputs[4], kv_grad, turned
        )

        @pl.when(row == 1)
        def _():
            make(kv_grad.at[4:8], kv_got.at[0:4], 6, partner).start()

    came(decays.at[0], 0)
    came(decays.at[1], 1)
    came(decays.at[2], 2)
    every = [decay_ref[0:1], decays[0, 0:1], decays[1, 0:1], decays[2, 0:1]]
    weights = []
    for step in range(4):
        factor = jnp.ones_like(every[0])
        for other in range(4):
            if other != step:
                later = (along - other + 4) % 4 > (along - step + 4) % 4
                factor = factor * jnp.where(later, every[other], 1.0)
        weights.append(factor)
    weight = jnp.ones_like(every[0])
    for step in (1, 2, 3):
        used = along >= step
        weights.append(jnp.where(used, weight, 0.0))
        weight = weight * jnp.where(used, every[step], 1.0)
    weights.append(weight)
    factors[...] = jnp.concatenate(weights, axis=0).T

    def add_up(chunk):
        def one(i, carry):
            head = chunk * (HM // 4) + i
            at = pl.ds(pl.multiple_of(head * HP, HP), HP)
            factor = factors[pl.ds(head, 1)]
            values = [got[slot, at].astype(F32) for slot in range(3)]
            earlier = factor[:, 4:5] * values[0]
            earlier = earlier + factor[:, 5:6] * values[1] + factor[:, 6:7] * values[2]
            out_ref[at] = earlier.astype(LOW)

            @pl.when(row == first_row)
            def _():
                whole = factor[:, 0:1] * own_ref[at].astype(F32)
                for slot in range(3):
                    whole = whole + factor[:, slot + 1 : slot + 2] * values[slot]
                total[at] = whole.astype(LOW)

            return carry

        lax.fori_loop(0, HM // 4, one, 0)

    def cross(chunk):
        return make(total.at[rows(chunk)], arriving.at[rows(chunk)], 19 + chunk, partner)

    def finish(chunk):
        add_up(chunk)

        @pl.when(row == first_row)
        def _():
            cross(chunk).start()

    came(got.at[2, rows(0)], 11)
    came(got.at[1, rows(0)], 15)
    finish(0)
    came(got.at[0, rows(2)], 9)
    came(got.at[1, rows(2)], 17)
    finish(2)
    came(got.at[0, rows(1)], 8)
    relay(1, 0, 16, up)
    came(got.at[2, rows(3)], 14)
    relay(3, 2, 18, down)
    if not forward:

        @pl.when(row == 0)
        def _():
            make(kv_grad.at[4:8], kv_got.at[0:4], 6, partner).wait_recv()
            kv_got[0:4] = (kv_grad[0:4].astype(F32) + kv_got[0:4].astype(F32)).astype(LOW)

        @pl.when(row == 1)
        def _():
            make(kv_grad.at[4:8], kv_got.at[0:4], 6, partner).wait_send()
            kv_got[0:4] = kv_grad[0:4]

        for slot, number, where in ((1, 3, up), (2, 4, opposite), (3, 5, down)):
            send(kv_got.at[slot], kv_got.at[3 + slot], number, where)
        inside_back_part(*inputs[:8], *outputs[:4], columns_ref, rows_ref)
    else:

        @pl.when(row == 1)
        def _():
            make(kv_out.at[0:4], kv_out.at[4:8], 6, partner).wait_recv()

        attention_part(lax.axis_index("fsdp"), inputs[0], kv_out, outputs[0])
        for block in range(4):
            downs[block].wait()
            outputs[1][:, block * BLOCK : (block + 1) * BLOCK] = mm(inputs[1][...], held[block])
    came(got.at[2, rows(1)], 12)
    came(got.at[1, rows(1)], 16)
    finish(1)
    came(got.at[0, rows(3)], 10)
    came(got.at[1, rows(3)], 18)
    finish(3)

    @pl.when(row == first_row)
    def _():
        for chunk in range(4):
            cross(chunk).wait_send()

    @pl.when(row != first_row)
    def _():
        for chunk in (0, 2, 1, 3):
            cross(chunk).wait_recv()

            def one(i, carry):
                head = chunk * (HM // 4) + i
                at = pl.ds(pl.multiple_of(head * HP, HP), HP)
                factor = factors[pl.ds(head, 1)]
                value = out_ref[at].astype(F32) + factor[:, 7:8] * arriving[at].astype(F32)
                out_ref[at] = value.astype(LOW)
                return carry

            lax.fori_loop(0, HM // 4, one, 0)

    if forward:

        @pl.when(row == 0)
        def _():
            make(kv_out.at[0:4], kv_out.at[4:8], 6, partner).wait_send()

    else:
        summed = kv_got[0].astype(F32)
        for slot in (1, 2, 3):
            came(kv_got.at[3 + slot], 2 + slot)
            summed = summed + kv_got[3 + slot].astype(F32)
        kv_out[...] = summed
    for copy in sent:
        copy.wait_send()


def exchange(contrib, decay, kv, direction, forward, extra, extra_outs):
    vmem = pl.BlockSpec(memory_space=pltpu.VMEM)
    dma = pltpu.SemaphoreType.DMA
    hbm = pl.BlockSpec(memory_space=pl.ANY)
    tokens = kv.shape[-2]
    held = (4, D, BLOCK) if forward else (1, 16, 128)
    blocks = (8, tokens, KV_WIDTH)
    kv_shape = (blocks, LOW) if forward else ((tokens, KV_WIDTH), F32)
    return pl.pallas_call(
        lambda *refs: exchange_kernel(direction, forward, *refs),
        out_shape=(
            jax.ShapeDtypeStruct((INNER_WIDTH, DS), LOW),
            jax.ShapeDtypeStruct(*kv_shape),
        )
        + tuple(jax.ShapeDtypeStruct(shape, kind) for shape, kind in extra_outs),
        in_specs=[vmem] * (2 + len(extra)) + [hbm if forward else vmem],
        out_specs=tuple([vmem] * (2 + len(extra_outs))),
        scratch_shapes=[
            pltpu.VMEM((3, INNER_WIDTH, DS), LOW),
            pltpu.VMEM((INNER_WIDTH, DS), LOW),
            pltpu.VMEM((INNER_WIDTH, DS), LOW),
            pltpu.VMEM((3, 8, HEADS_WIDE), F32),
            pltpu.VMEM((HEADS_WIDE, 8), F32),
            pltpu.VMEM(blocks, LOW),
            pltpu.VMEM((tokens, HEADS_WIDE), F32),
            pltpu.VMEM((HEADS_WIDE, tokens), F32),
            pltpu.VMEM(blocks, LOW),
            pltpu.VMEM((KV_WIDTH, 8 * tokens), F32),
            pltpu.VMEM(held, LOW),
            dma((4,)),
            dma((23,)),
            dma((23,)),
        ],
        compiler_params=pltpu.CompilerParams(
            collective_id=3 if forward else 4,
            has_side_effects=True,
            vmem_limit_bytes=28 * 1024 * 1024,
        ),
        name="exchange_forward" if forward else "exchange_back",
    )(contrib, decay, kv, *extra)


def mixer_part(
    proj_ref,
    xs_ref,
    bc_ref,
    cum_ref,
    step_ref,
    heads_ref,
    gain_ref,
    state_ref,
    y_ref,
    cross_ref,
    low_ref,
):
    tokens = xs_ref.shape[0]
    cum, step = (cum_ref[...], step_ref[...])
    cum_rows, step_rows = (cum.T, step.T)
    bmat, cmat = (bc_ref[:, :DS], bc_ref[:, DS:])
    correlation = mm(cmat, bmat, 1, 1)
    lower = lower_ones(tokens) > 0.0
    lane = lax.broadcasted_iota(jnp.int32, (tokens, 128), 1)
    heads = head_map()
    cross = mm(cmat, state_ref[...], 1, 1) * widen(jnp.exp(cum), heads)
    cross_ref[...] = cross
    skip = widen(jnp.broadcast_to(heads_ref[2:3], (8, HEADS_WIDE)), heads)[0:1]
    for pair in range(HM // 2):
        lanes = slice(pair * 128, (pair + 1) * 128)
        xs = xs_ref[:, lanes]
        kernels = []
        for head in (2 * pair, 2 * pair + 1):
            fading = fading_of(cum, cum_rows, head, lower)
            kernels.append((fading * correlation * step_rows[head : head + 1]).astype(LOW))
        zero = jnp.zeros_like(xs)
        split = jnp.concatenate([jnp.where(lane < HP, xs, zero), jnp.where(lane < HP, zero, xs)])
        inside = mm(jnp.concatenate(kernels, axis=1), split)
        y_ref[:, lanes] = inside + cross_ref[:, lanes] + skip[:, lanes] * xs.astype(F32)
    gate = proj_ref[AHEAD:, :INNER_WIDTH]
    gated = y_ref[...] * (gate * jax.nn.sigmoid(gate))
    scale = lax.rsqrt(jnp.mean(gated * gated, axis=1, keepdims=True) + EPS)
    low_ref[:, :INNER_WIDTH] = (gated * scale * gain_ref[...]).astype(LOW)


def mixer_back_kernel(
    proj_ref,
    grad_ref,
    y_ref,
    cross_ref,
    xs_ref,
    bc_ref,
    cum_ref,
    gain_ref,
    dy_ref,
    dz_ref,
    contrib_ref,
    cum_grad_ref,
    gain_grad_ref,
    skip_grad_ref,
):
    tokens = xs_ref.shape[0]
    gate, y, grad = (proj_ref[AHEAD:, :INNER_WIDTH], y_ref[...], grad_ref[:, :INNER_WIDTH])
    sigmoid = jax.nn.sigmoid(gate)
    opened = gate * sigmoid
    gated = y * opened
    scale = lax.rsqrt(jnp.mean(gated * gated, axis=1, keepdims=True) + EPS)
    normal = gated * scale
    gain_grad_ref[...] = jnp.sum(grad * normal, axis=0, keepdims=True)
    inner = grad * gain_ref[...]
    dgated = scale * (inner - normal * jnp.mean(inner * normal, axis=1, keepdims=True))
    dz_ref[...] = (dgated * y * (sigmoid * (1.0 + gate * (1.0 - sigmoid)))).astype(LOW)
    dy = dgated * opened
    dy_ref[...] = dy
    heads = head_map()
    cum = cum_ref[...]
    cross_grad = (dy * widen(jnp.exp(cum), heads)).astype(LOW)
    contrib_ref[...] = mm(cross_grad, bc_ref[:, DS:], 0, 0).astype(LOW)
    cum_grad_ref[...] = per_head(dy * cross_ref[...], heads)
    used = jnp.sum(dy * xs_ref[...].astype(F32), axis=0, keepdims=True)
    skip_grad_ref[...] = per_head(jnp.broadcast_to(used, (8, INNER_WIDTH)), heads)[0:1]


def inside_back_part(
    dy_ref,
    xs_ref,
    bc_ref,
    cum_ref,
    step_ref,
    heads_ref,
    state_ref,
    cum_grad_in_ref,
    dxs_ref,
    dbc_ref,
    cum_grad_ref,
    step_grad_ref,
    columns_ref,
    rows_ref,
):
    tokens = xs_ref.shape[0]
    cum, step = (cum_ref[...], step_ref[...])
    cum_rows, step_rows = (cum.T, step.T)
    bmat, cmat = (bc_ref[:, :DS], bc_ref[:, DS:])
    correlation = mm(cmat, bmat, 1, 1)
    lower = lower_ones(tokens) > 0.0
    lane = lax.broadcasted_iota(jnp.int32, (tokens, 128), 1)
    heads = head_map()
    skip = widen(jnp.broadcast_to(heads_ref[2:3], (8, HEADS_WIDE)), heads)[0:1]
    grad_correlation = jnp.zeros((tokens, tokens), F32)
    columns = jnp.zeros((tokens, HEADS_WIDE), F32)
    rows_ref[...] = jnp.zeros_like(rows_ref)
    for pair in range(HM // 2):
        lanes = slice(pair * 128, (pair + 1) * 128)
        xs = xs_ref[:, lanes]
        dy = dy_ref[:, lanes]
        dy_low = dy.astype(LOW)
        zero = jnp.zeros_like(dy_low)
        split = jnp.concatenate(
            [jnp.where(lane < HP, dy_low, zero), jnp.where(lane < HP, zero, dy_low)]
        )
        grads = mm(split, xs, 1, 1)
        kernels = []
        for i in range(2):
            head = 2 * pair + i
            fading = fading_of(cum, cum_rows, head, lower)
            row = step_rows[head : head + 1]
            shaped = fading * correlation
            kernels.append((shaped * row).astype(LOW))
            grad = grads[i * tokens : (i + 1) * tokens]
            grad_correlation = grad_correlation + grad * fading * row
            product = grad * shaped
            rows_ref[head : head + 1] = jnp.sum(product, axis=0, keepdims=True)
            summed = jnp.sum(product * row, axis=1, keepdims=True)
            columns = columns + jnp.where(lane == head, summed, 0.0)
        dxs = mm(jnp.concatenate(kernels), split, 0, 0)
        dxs_ref[:, lanes] = dxs + skip[:, lanes] * dy
    columns_ref[...] = columns
    grad_low = grad_correlation.astype(LOW)
    dbc_ref[:, :DS] = mm(grad_low, cmat, 0, 0)
    cross_grad = (dy_ref[...] * widen(jnp.exp(cum), heads)).astype(LOW)
    dbc_ref[:, DS:] = mm(grad_low, bmat) + mm(cross_grad, state_ref[...])
    step_grad = rows_ref[...].T
    step_grad_ref[...] = step_grad
    cum_grad_ref[...] = cum_grad_in_ref[...] + columns_ref[...] - step * step_grad


def state_back_part(
    proj_ref,
    dt_ref,
    taps_ref,
    bias_ref,
    heads_ref,
    xs_ref,
    bc_ref,
    cum_ref,
    step_ref,
    dxs_ref,
    dbc_ref,
    cum_grad_ref,
    step_grad_ref,
    state_ref,
    leaving_ref,
    dxbc_ref,
    returned_ref,
    ddt_ref,
    taps_grad_ref,
    bias_grad_ref,
    heads_grad_ref,
    extended,
    flowing,
):
    tokens = xs_ref.shape[0]
    heads = head_map()
    cum, step = (cum_ref[...], step_ref[...])
    products = []
    for head in range(HM):
        rows = slice(head * HP, (head + 1) * HP)
        value = leaving_ref[rows].astype(F32)
        products.append(jnp.sum(value * state_ref[rows].astype(F32), axis=0, keepdims=True))
    products.append(jnp.zeros((HEADS_WIDE - HM, DS), F32))
    decay_grad = jnp.sum(jnp.concatenate(products).T, axis=0, keepdims=True)
    last = cum[tokens - 1 : tokens]
    fading = jnp.exp(last - cum)
    tail = fading * step
    wide_tail = widen(tail, heads)
    xs = xs_ref[...].astype(F32)
    reached = mm(bc_ref[:, :DS], leaving_ref[...], 1, 1)
    dact_xs = dxs_ref[...] + wide_tail * reached
    db = dbc_ref[:, :DS] + mm((xs * wide_tail).astype(LOW), leaving_ref[...])
    tail_grad = per_head(xs * reached, heads)
    step_grad = step_grad_ref[...] + tail_grad * fading
    moved = tail_grad * tail
    cum_grad = cum_grad_ref[...] - moved
    row = lax.broadcasted_iota(jnp.int32, (tokens, HEADS_WIDE), 0)
    at_last = jnp.sum(moved, axis=0, keepdims=True) + decay_grad * jnp.exp(last)
    cum_grad = cum_grad + jnp.where(row == tokens - 1, at_last, 0.0)
    log_grad = mm(lower_ones(tokens), cum_grad, 0, 0, precision=HIGHEST_PRECISION)
    rate = -jnp.exp(heads_ref[1:2])
    total_step = step_grad + log_grad * rate
    ddt = total_step * jax.nn.sigmoid(dt_ref[AHEAD:] + heads_ref[0:1])
    ddt_ref[...] = ddt.astype(LOW)
    heads_grad_ref[0:1] = jnp.sum(ddt, axis=0, keepdims=True)
    heads_grad_ref[1:2] = jnp.sum(log_grad * step * rate, axis=0, keepdims=True)
    heads_grad_ref[2:8] = jnp.zeros((6, HEADS_WIDE), F32)

    channels = slice(INNER_WIDTH, INNER_WIDTH + CONV_CHANNELS)
    convolved = convolve(
        extended, proj_ref[AHEAD:, channels], proj_ref[AHEAD - 8 : AHEAD, channels], taps_ref, bias_ref
    )
    sigmoid = jax.nn.sigmoid(convolved)
    slope = sigmoid * (1.0 + convolved * (1.0 - sigmoid))
    dact = jnp.concatenate([dact_xs, db, dbc_ref[:, DS:]], axis=1)
    dconv = dact * slope
    bias_grad_ref[...] = jnp.sum(dconv, axis=0, keepdims=True)
    for tap in range(KW):
        taps_grad_ref[tap : tap + 1] = jnp.sum(
            dconv * extended[5 + tap : 5 + tap + tokens], axis=0, keepdims=True
        )
    flowing[0:8] = jnp.zeros((8, CONV_CHANNELS), F32)
    flowing[8 : 8 + tokens] = dconv
    flowing[8 + tokens : 16 + tokens] = jnp.zeros((8, CONV_CHANNELS), F32)
    total = taps_ref[3:4] * dconv
    early = jnp.zeros((8, CONV_CHANNELS), F32)
    for tap in range(3):
        total = total + taps_ref[tap : tap + 1] * flowing[11 - tap : 11 - tap + tokens]
        early = early + taps_ref[tap : tap + 1] * flowing[3 - tap : 11 - tap]
    dxbc_ref[...] = total
    returned_ref[...] = early


def last_kernel(
    proj_ref,
    dt_ref,
    taps_ref,
    bias_ref,
    heads_ref,
    xs_ref,
    bc_ref,
    cum_ref,
    step_ref,
    state_ref,
    leaving_ref,
    dxs_ref,
    dbc_ref,
    cum_grad_ref,
    step_grad_ref,
    kv_ref,
    cosine_ref,
    sine_ref,
    skip_grad_ref,
    dq_ref,
    dxbc_ref,
    returned_ref,
    ddt_ref,
    taps_grad_ref,
    bias_grad_ref,
    heads_row_ref,
    kv_low_ref,
    dq_low_ref,
    heads_grad_ref,
    extended,
    flowing,
):
    half = KV_WIDTH // 2
    kv = kv_ref[...]
    kv_low_ref[:, :half] = rotate(kv[:, :half], cosine_ref[...], -sine_ref[...]).astype(LOW)
    kv_low_ref[:, half:] = kv[:, half:].astype(LOW)
    dq_low_ref[...] = rotate(dq_ref[...], cosine_ref[...], -sine_ref[...]).astype(LOW)
    state_back_part(
        proj_ref,
        dt_ref,
        taps_ref,
        bias_ref,
        heads_ref,
        xs_ref,
        bc_ref,
        cum_ref,
        step_ref,
        dxs_ref,
        dbc_ref,
        cum_grad_ref,
        step_grad_ref,
        state_ref,
        leaving_ref,
        dxbc_ref,
        returned_ref,
        ddt_ref,
        taps_grad_ref,
        bias_grad_ref,
        heads_grad_ref,
        extended,
        flowing,
    )

    def moved(row, by):
        return pltpu.roll(jnp.broadcast_to(row, (8, HEADS_WIDE)), by, 1)[0:1]

    heads = heads_grad_ref[0:1] + moved(heads_grad_ref[1:2], HM)
    heads_row_ref[...] = heads + moved(skip_grad_ref[...], 2 * HM)


def probabilities(query, keys, allowed):
    scores = mm(query, keys, 1, 1) * HEAD_SIZE ** (-0.5)
    masked = jnp.where(allowed, scores, -1e30)
    peak = jnp.max(masked, axis=1, keepdims=True)
    expo = jnp.exp(masked - peak)
    return expo / jnp.sum(expo, axis=1, keepdims=True)


def allowed_keys(rank, tokens):
    row, column = (rank // 4, rank % 4)
    at = lax.broadcasted_iota(jnp.int32, (tokens, 8 * tokens), 0)
    lane = lax.broadcasted_iota(jnp.int32, (tokens, 8 * tokens), 1)
    block = lane // tokens
    near = jnp.where(block == 0, jnp.where(lane <= at, 1, 0), jnp.where(block <= column, 1, 0))
    return jnp.where(block < 4, near, row) > 0


def attention_part(rank, query_ref, kvs_ref, out_ref):
    tokens = query_ref.shape[0]
    allowed = allowed_keys(rank, tokens)
    kv = kvs_ref[...].reshape(8 * tokens, KV_WIDTH)
    half = KV_WIDTH // 2
    group_size = QUERY_HEADS // KEY_VALUE_HEADS
    results = []
    for head in range(QUERY_HEADS):
        group = head // group_size
        keys = kv[:, group * HEAD_SIZE : (group + 1) * HEAD_SIZE]
        values = kv[:, half + group * HEAD_SIZE : half + (group + 1) * HEAD_SIZE]
        query = query_ref[:, head * HEAD_SIZE : (head + 1) * HEAD_SIZE]
        weights = probabilities(query, keys, allowed).astype(LOW)
        results.append(mm(weights, values).astype(LOW))
        if head % 2 == 1:
            lanes = slice((head - 1) * HEAD_SIZE, (head + 1) * HEAD_SIZE)
            out_ref[:, lanes] = jnp.concatenate(results[-2:], axis=1)


def attention_back_part(
    rank, query_ref, kvs_ref, grad_ref, dq_ref, dkv_ref, turned
):
    tokens = query_ref.shape[0]
    allowed = allowed_keys(rank, tokens)
    kv = kvs_ref[...].reshape(8 * tokens, KV_WIDTH)
    half = KV_WIDTH // 2
    group_size = QUERY_HEADS // KEY_VALUE_HEADS
    scale = HEAD_SIZE ** (-0.5)
    for group in range(KEY_VALUE_HEADS):
        keys = kv[:, group * HEAD_SIZE : (group + 1) * HEAD_SIZE]
        values = kv[:, half + group * HEAD_SIZE : half + (group + 1) * HEAD_SIZE]
        dkeys = jnp.zeros((HEAD_SIZE, 8 * tokens), F32)
        dvalues = jnp.zeros((HEAD_SIZE, 8 * tokens), F32)
        results = []
        for head in range(group * group_size, (group + 1) * group_size):
            query = query_ref[:, head * HEAD_SIZE : (head + 1) * HEAD_SIZE]
            start = INNER_WIDTH + head * HEAD_SIZE
            grad = grad_ref[:, start : start + HEAD_SIZE].astype(LOW)
            weights = probabilities(query, keys, allowed)
            dweights = mm(grad, values, 1, 1)
            inner = jnp.sum(dweights * weights, axis=1, keepdims=True)
            dscores = (weights * (dweights - inner)).astype(LOW)
            dvalues = dvalues + mm(grad, weights.astype(LOW), 0, 0)
            dkeys = dkeys + mm(query, dscores, 0, 0)
            results.append(mm(dscores, keys) * scale)
            if head % 2 == 1:
                lanes = slice((head - 1) * HEAD_SIZE, (head + 1) * HEAD_SIZE)
                pair = jnp.concatenate(results[-2:], axis=1)
                dq_ref[:, lanes] = pair
        turned[group * HEAD_SIZE : (group + 1) * HEAD_SIZE] = dkeys * scale
        turned[half + group * HEAD_SIZE : half + (group + 1) * HEAD_SIZE] = dvalues
    dkv_ref[...] = turned[...].T.astype(LOW).reshape(dkv_ref.shape)


def middle_kernel(
    proj_ref,
    attended_ref,
    xs_ref,
    bc_ref,
    cum_ref,
    step_ref,
    heads_ref,
    gain_ref,
    state_ref,
    y_ref,
    cross_ref,
    joined_ref,
):
    joined_ref[:, INNER_WIDTH:] = attended_ref[...]
    mixer_part(
        proj_ref,
        xs_ref,
        bc_ref,
        cum_ref,
        step_ref,
        heads_ref,
        gain_ref,
        state_ref,
        y_ref,
        cross_ref,
        joined_ref,
    )


BLOCK = 512


def stream(weights_ref, held_ref, sems, start):
    copies = []
    for block in range(held_ref.shape[0]):
        copy = pltpu.make_async_copy(
            weights_ref.at[:, pl.ds(start + block * BLOCK, BLOCK)],
            held_ref.at[block],
            sems.at[block],
        )
        copy.start()
        copies.append(copy)
    return copies


def feed_forward_kernel(
    weights_ref,
    joined_ref,
    hidden_in_ref,
    grad_ref,
    dhidden_ref,
    gain_ref,
    second_ref,
    rest_ref,
    output_ref,
    dmid_ref,
    mid_low_ref,
    djoined_ref,
    gain_grad_ref,
    join_held,
    gate_held,
    down_held,
    join_sem,
    gate_sem,
    down_sem,
):
    joins = stream(weights_ref, join_held, join_sem, MIX_IN + 2 * FF)
    gates = stream(weights_ref, gate_held, gate_sem, MIX_IN)
    downs = stream(weights_ref, down_held, down_sem, COLS - FF)
    mid = hidden_in_ref[...]
    for block in range(4):
        joins[block].wait()
        lanes = slice(block * BLOCK, (block + 1) * BLOCK)
        mid = mid + mm(joined_ref[:, lanes], join_held[block], 1, 1)
    rest_ref[:, 2 * FF : 2 * FF + INNER_WIDTH + Q_WIDTH] = joined_ref[...]
    output_ref[...] = mid
    scale = lax.rsqrt(jnp.mean(mid * mid, axis=1, keepdims=True) + EPS)
    second = (mid * scale * gain_ref[...]).astype(LOW)
    second_ref[...] = second
    dsecond = jnp.zeros(mid.shape, F32)
    for block in range(4):
        lanes = slice(block * BLOCK, (block + 1) * BLOCK)
        far = slice(FF + block * BLOCK, FF + (block + 1) * BLOCK)
        gates[block].wait()
        gate = mm(second, gate_held[block])
        gates[4 + block].wait()
        up = mm(second, gate_held[4 + block])
        sigmoid = jax.nn.sigmoid(gate)
        opened = gate * sigmoid
        hidden = (opened * up).astype(LOW)
        at = 2 * FF + INNER_WIDTH + Q_WIDTH + block * BLOCK
        rest_ref[:, at : at + BLOCK] = hidden
        downs[block].wait()
        output_ref[...] += mm(hidden, down_held[block], 1, 1)
        dhidden = dhidden_ref[:, lanes]
        dgate = (dhidden * up * (sigmoid * (1.0 + gate * (1.0 - sigmoid)))).astype(LOW)
        dup = (dhidden * opened).astype(LOW)
        rest_ref[:, lanes] = dgate
        rest_ref[:, far] = dup
        dsecond = dsecond + mm(dgate, gate_held[block], 1, 1)
        dsecond = dsecond + mm(dup, gate_held[4 + block], 1, 1)
    normal = mid * scale
    gain_grad_ref[...] = jnp.sum(dsecond * normal, axis=0, keepdims=True)
    inner = dsecond * gain_ref[...]
    dmid = grad_ref[...] + scale * (
        inner - normal * jnp.mean(inner * normal, axis=1, keepdims=True)
    )
    dmid_ref[...] = dmid
    mid_low = dmid.astype(LOW)
    mid_low_ref[...] = mid_low
    for block in range(4):
        djoined_ref[:, block * BLOCK : (block + 1) * BLOCK] = mm(mid_low, join_held[block])


def closing_kernel(
    weights_ref,
    dz_ref,
    dxbc_ref,
    returning_ref,
    dq_ref,
    kv_ref,
    rest_ref,
    dt_ref,
    dt_weights_ref,
    first_ref,
    hidden_in_ref,
    scale_ref,
    gain_ref,
    dmid_ref,
    mid_gain_ref,
    mixer_gain_ref,
    taps_grad_ref,
    bias_grad_ref,
    heads_row_ref,
    out_ref,
    input_grad_ref,
    small_ref,
    held,
    returned,
    sems,
    row_sem,
):
    copies = stream(weights_ref, held, sems, 0)
    rep, rank = (lax.axis_index("rep"), lax.axis_index("fsdp"))
    after, ahead = ((rep, (rank + 1) % 8), (rep, (rank + 7) % 8))
    greet([after, ahead])
    back = push(returning_ref, returned, row_sem.at[0], row_sem.at[1], ahead)
    back.start()

    def put(start, row):
        for i in range(row.shape[1] // 128):
            small_ref[start + i : start + i + 1] = row[:, i * 128 : (i + 1) * 128]

    tokens = dz_ref.shape[0]
    stop = INNER_WIDTH + CONV_CHANNELS
    out_ref[:, :INNER_WIDTH] = dz_ref[...]
    out_ref[:, stop : stop + Q_WIDTH] = dq_ref[...]
    out_ref[:, stop + Q_WIDTH : MIX_IN] = kv_ref[...]
    out_ref[:, MIX_IN:] = rest_ref[...]
    out_ref[0 : tokens - 16, INNER_WIDTH:stop] = dxbc_ref[0 : tokens - 16].astype(LOW)
    dfirst = mm(dt_ref[:, :HM], dt_weights_ref[...], 1, 1)

    def through(block):
        copies[block].wait()
        lanes = slice(block * BLOCK, (block + 1) * BLOCK)
        return mm(out_ref[:, lanes], held[block], 1, 1)

    for block in (0, 1, 2, 7):
        dfirst = dfirst + through(block)
    back.wait_recv()
    late = jnp.where(rank < 7, returned[...], 0.0)
    late = jnp.concatenate([jnp.zeros_like(late), late])
    tail = dxbc_ref[tokens - 16 : tokens]
    out_ref[tokens - 16 : tokens, INNER_WIDTH:stop] = (tail + late).astype(LOW)
    for block in (3, 4, 5, 6):
        dfirst = dfirst + through(block)
    scale = jnp.max(scale_ref[...], axis=1, keepdims=True)
    normal = hidden_in_ref[...] * scale
    put(0, jnp.sum(dfirst * normal, axis=0, keepdims=True))
    inner = dfirst * gain_ref[...]
    input_grad_ref[...] = dmid_ref[...] + scale * (
        inner - normal * jnp.mean(inner * normal, axis=1, keepdims=True)
    )
    put(D // 128, mid_gain_ref[...])
    put(2 * D // 128, mixer_gain_ref[...])
    start = (2 * D + INNER_WIDTH) // 128
    for tap in range(KW):
        put(start + tap * CONV_CHANNELS // 128, taps_grad_ref[tap : tap + 1])
    start = start + KW * CONV_CHANNELS // 128
    put(start, bias_grad_ref[...])
    put(HEADS_ROW, heads_row_ref[...])
    small_ref[HEADS_ROW + 1 : STEP_ROW] = jnp.zeros((STEP_ROW - HEADS_ROW - 1, 128), F32)
    steps = mm(dt_ref[...], first_ref[AHEAD:], 0, 0)
    for part in range(8):
        at = STEP_ROW + part * HM
        small_ref[at : at + HM] = steps[0:HM, part * 128 : (part + 1) * 128]
    at = STEP_ROW + 8 * HM
    small_ref[at:SMALL_ROWS] = jnp.zeros((SMALL_ROWS - at, 128), F32)
    back.wait_send()


def local_call(kernel, outs, args, scratch=(), scalars=0, streams=0, sems=(), grant=16, meeting=None):
    vmem = pl.BlockSpec(memory_space=pltpu.VMEM)
    smem = pl.BlockSpec(memory_space=pltpu.SMEM)
    hbm = pl.BlockSpec(memory_space=pl.ANY)
    return pl.pallas_call(
        kernel,
        out_shape=tuple(jax.ShapeDtypeStruct(shape, kind) for shape, kind in outs),
        in_specs=[smem] * scalars + [hbm] * streams + [vmem] * (len(args) - scalars - streams),
        out_specs=tuple([vmem] * len(outs)),
        scratch_shapes=[pltpu.VMEM(shape, kind) for shape, kind in scratch]
        + [pltpu.SemaphoreType.DMA((count,)) for count in sems],
        compiler_params=pltpu.CompilerParams(
            vmem_limit_bytes=grant * 1024 * 1024,
            collective_id=meeting,
            has_side_effects=meeting is not None,
        ),
        name=kernel.__name__,
    )(*args)


def sigmoid_linear(value_rows):
    return value_rows * jax.nn.sigmoid(value_rows)


def shards(hidden_in, cotangent, units, unit_momentum, small, small_momentum):
    sequence_count, tokens, width = hidden_in.shape
    rank = lax.axis_index("fsdp").astype(jnp.int32)
    flat_in = hidden_in.reshape(tokens, width)
    grad_out = cotangent.reshape(tokens, width)
    gain_in = small[:D]
    weights, first_rows, out_low, scale_in, cosine, sine = gather_weights(
        units, flat_in, grad_out, gain_in.reshape(1, width)
    )
    w_mix = weights[:, :MIX_IN]

    def times(a, b):
        return jnp.dot(a, b, preferred_element_type=jnp.float32)

    gain_mid = small[D : 2 * D]
    small_rows = jnp.pad(small[: 99 * 128], (0, 5 * 128)).reshape(104, 128)
    dt_proj = small[SMALL_SIZE - D * HM :].reshape(D, HM)
    dt_narrow = dt_proj.astype(jnp.bfloat16)
    dt_weights = jnp.pad(dt_narrow, ((0, 0), (0, HEADS_WIDE - HM)))
    projected = times(first_rows, w_mix)
    dt_raw = times(first_rows, dt_weights)
    wide = (tokens, INNER_WIDTH)
    per_head_shape = (tokens, HEADS_WIDE)
    state_shape = (INNER_WIDTH, DS)
    extended_shape = ((tokens + 8, CONV_CHANNELS), F32)
    (
        query,
        local_kv,
        xs,
        bc,
        cum,
        step,
        contrib,
        decay,
        taps,
        bias_row,
        heads,
        gain_row,
    ) = local_call(
        front_kernel,
        [
            ((tokens, Q_WIDTH), LOW),
            ((tokens, KV_WIDTH), LOW),
            (wide, LOW),
            ((tokens, 2 * DS), LOW),
            (per_head_shape, F32),
            (per_head_shape, F32),
            (state_shape, LOW),
            ((8, HEADS_WIDE), F32),
            ((KW, CONV_CHANNELS), F32),
            ((1, CONV_CHANNELS), F32),
            ((8, HEADS_WIDE), F32),
            ((1, INNER_WIDTH), F32),
        ],
        [projected, dt_raw, small_rows, cosine, sine],
        [extended_shape],
    )
    state_in, kvs, attended, dhidden = exchange(
        contrib,
        decay,
        local_kv,
        1,
        True,
        [query, out_low, weights],
        [((tokens, Q_WIDTH), LOW), ((tokens, FF), F32)],
    )
    y, cross, joined_low = local_call(
        middle_kernel,
        [(wide, F32), (wide, F32), ((tokens, INNER_WIDTH + Q_WIDTH), LOW)],
        [projected, attended, xs, bc, cum, step, heads, gain_row, state_in],
    )
    flat = (tokens, width)
    (
        second,
        rest,
        output,
        grad_mid,
        mid_low,
        grad_joined,
        grad_gain_mid,
    ) = local_call(
        feed_forward_kernel,
        [
            (flat, LOW),
            ((tokens, COLS - MIX_IN), LOW),
            (flat, F32),
            (flat, F32),
            (flat, LOW),
            ((tokens, INNER_WIDTH + Q_WIDTH), F32),
            ((1, width), F32),
        ],
        [weights, joined_low, flat_in, grad_out, dhidden, gain_mid.reshape(1, width)],
        [((4, D, BLOCK), LOW), ((8, D, BLOCK), LOW), ((4, D, BLOCK), LOW)],
        streams=1,
        sems=(4, 8, 4),
        grant=44,
    )
    dy, dz, contrib_back, cross_cum, grad_gain_mixer, grad_skip = local_call(
        mixer_back_kernel,
        [
            (wide, F32),
            (wide, LOW),
            (state_shape, LOW),
            (per_head_shape, F32),
            ((1, INNER_WIDTH), F32),
            ((1, HEADS_WIDE), F32),
        ],
        [projected, grad_joined, y, cross, xs, bc, cum, gain_row],
    )
    leaving, kv_total, dxs, dbc, cum_grad, step_grad, grad_query = exchange(
        contrib_back,
        decay,
        kvs,
        -1,
        False,
        [dy, xs, bc, cum, step, heads, state_in, cross_cum, query, grad_joined],
        [
            (wide, F32),
            ((tokens, 2 * DS), F32),
            (per_head_shape, F32),
            (per_head_shape, F32),
            ((tokens, Q_WIDTH), F32),
        ],
    )
    dxbc, returning, dt_low, grad_taps, grad_conv_bias, heads_row, kv_low, dq_low = local_call(
        last_kernel,
        [
            ((tokens, CONV_CHANNELS), F32),
            ((8, CONV_CHANNELS), F32),
            (per_head_shape, LOW),
            ((KW, CONV_CHANNELS), F32),
            ((1, CONV_CHANNELS), F32),
            ((1, HEADS_WIDE), F32),
            ((tokens, KV_WIDTH), LOW),
            ((tokens, Q_WIDTH), LOW),
        ],
        [
            projected,
            dt_raw,
            taps,
            bias_row,
            heads,
            xs,
            bc,
            cum,
            step,
            state_in,
            leaving,
            dxs,
            dbc,
            cum_grad,
            step_grad,
            kv_total,
            cosine,
            sine,
            grad_skip,
            grad_query,
        ],
        [((8, HEADS_WIDE), F32), extended_shape, ((tokens + 16, CONV_CHANNELS), F32)],
    )
    columns, grad_input, local_small = local_call(
        closing_kernel,
        [
            ((tokens, COLS), LOW),
            (flat, F32),
            ((SMALL_ROWS, 128), F32),
        ],
        [
            weights,
            dz,
            dxbc,
            returning,
            dq_low,
            kv_low,
            rest,
            dt_low,
            dt_narrow,
            first_rows,
            flat_in,
            scale_in,
            gain_in.reshape(1, width),
            grad_mid,
            grad_gain_mid,
            grad_gain_mixer,
            grad_taps,
            grad_conv_bias,
            heads_row,
        ],
        [((8, D, BLOCK), LOW), ((8, CONV_CHANNELS), F32)],
        streams=1,
        sems=(8, 2),
        grant=44,
        meeting=5,
    )
    output = output.reshape(sequence_count, tokens, width)
    grad_input = grad_input.reshape(sequence_count, tokens, width)
    owned, small_grad = reduce_gradients(
        first_rows,
        second,
        mid_low,
        out_low,
        columns,
        local_small.reshape(2, SMALL_HALF, 128),
    )
    rows = small_grad.reshape(SMALL_ROWS, 128)
    steps = rows[STEP_ROW : STEP_ROW + 8 * HM].reshape(8, HM, 128).transpose(0, 2, 1)
    small_grad = jnp.concatenate(
        [rows[:HEADS_ROW].reshape(-1), rows[HEADS_ROW, : 3 * HM], steps.reshape(-1)]
    )
    momentum_new = MOM_MAT * unit_momentum + owned.reshape(12, D, UCOL).astype(F32)
    replica = lax.axis_index("rep").astype(jnp.int32)
    layer = replica // 2 % 4
    chosen = jnp.stack([3 * layer + 2 * (replica % 2), 3 * layer + 1])
    ortho = spread_blocks(orthogonalize_two(momentum_new, chosen))
    ortho = ortho.reshape(12, D, UCOL).astype(F32)
    units_new = units.astype(jnp.float32) * (1.0 - RATE_MAT * DECAY_MAT) - RATE_MAT * ortho
    small_momentum_new = MOM_VEC * small_momentum + small_grad
    token_total = lax.axis_size("rep") * SEQS * LEN
    small_new = small - RATE_VEC / math.sqrt(token_total) * small_momentum_new
    return (output, grad_input, units_new, momentum_new, small_new, small_momentum_new)


def solution(mesh):
    placed = (
        P("rep", "fsdp", None),
        P("rep", "fsdp", None),
        P("fsdp", None, None),
        P("fsdp", None, None),
        P(),
        P(),
    )
    return jax.shard_map(
        shards,
        mesh=mesh,
        in_specs=placed,
        out_specs=(
            P("rep", "fsdp", None),
            P("rep", "fsdp", None),
            P("fsdp", None, None),
            P("fsdp", None, None),
            P(),
            P(),
        ),
        check_vma=False,
    )
```
